256 devices in a mesh: grp: 8 (over y, core), row: 32 (over x, z).
Axes of the slice: x: 4, y: 4, z: 8, core: 2. Of those that a mesh axis runs over, the one named last changes fastest.
Arguments:
- labeled: bfloat16 [4, 1024, 1024], P(None, 'row', 'grp'), may hold values from -6 to 6
- candidates: bfloat16 [8192, 1024], P(('grp', 'row')), may hold values from -6 to 6
- factor_rows: bfloat16 [4, 1024, 4096], P(None, 'row'), may hold values from -6 to 6
- block_inverse: bfloat16 [4, 1024, 1024], P(None, 'row'), as said below
Outputs:
- whitened: bfloat16 [4, 1024, 8192], P(None, 'row', 'grp')
- explained: float32 [8192], P('grp')
The draws below stay inside these ranges and needn't reach their ends.
Inputs may be any that keep to these rules, and one draw needn't show every extreme that they name: Each block of block_inverse is lower triangular with a positive diagonal; it is given as is and is not derived from factor_rows.
All inputs are finite; a program needn't handle non-finite values.
Results may differ from the reference program's by a relative error of at most 0.0075.
Values may be sent and summed in bfloat16 or wider, within the bound.
A program may use at most 64 MiB of HBM per device.

```python
import math
import jax
import jax.numpy as jnp
from jax import lax

F = 1024
B = 1024
NB = 4
NC = 8192
N = 4096


def draw_block_inverse(key, part):
    key_scale = jax.random.fold_in(key, 11)
    key_noise = jax.random.fold_in(key, 12)
    position = jnp.arange(B).astype(jnp.float32)
    base = jnp.exp(jax.random.uniform(key_scale, (NB, B), jnp.float32, math.log(1.0 / 150.0), math.log(1.0 / 60.0)))
    base = base * jnp.exp(math.log(3.0) * position / B)[None, :]
    noise = jax.random.normal(key_noise, (NB, B, B), jnp.float32)
    lower = (position[:, None] > position[None, :]).astype(jnp.float32)
    diagonal = (position[:, None] == position[None, :]).astype(jnp.float32)
    spread = 0.3 / jnp.sqrt(position + 1.0)
    entries = noise * lower[None] * (base * spread[None, :])[:, :, None] + diagonal[None] * base[:, :, None]
    return entries.astype(jnp.bfloat16)


def block_levels(stream_key, shape, cuts, low, top_value):
    factor_of = 1.0
    for axis_at, blocks in cuts:
        steps = jax.random.uniform(jax.random.fold_in(jax.random.fold_in(stream_key, 6), axis_at), (blocks,), jnp.float32, low / len(cuts), top_value / len(cuts))
        factor_of = factor_of * jnp.repeat(jnp.exp(steps), shape[axis_at] // blocks).reshape((-1,) + (1,) * (len(shape) - 1 - axis_at))
    return factor_of


def bell_draw(stream_key, extent, scale, limit, pieces=(), kind=jnp.bfloat16):
    loudness = block_levels(stream_key, extent, pieces, -0.22, 0.18) if pieces else 1.0
    drawn = jax.random.normal(stream_key, extent, jnp.float32) * scale * loudness
    return jnp.minimum(jnp.maximum(drawn, -limit), limit).astype(kind)


def setup_inputs(seed: int = 0) -> dict:
    splits = jax.random.split(jax.random.key(seed), 5)
    return {
        "labeled": bell_draw(splits[0], (NB, B, F), 1.0, 6.0, ((1, 32), (2, 8))),
        "candidates": bell_draw(splits[1], (NC, F), 1.0, 6.0, ((0, 256),)),
        "factor_rows": bell_draw(splits[2], (NB, B, N), 1.0, 6.0, ((1, 32),)),
        "block_inverse": draw_block_inverse(jax.random.fold_in(splits[4], 71), 0),
    }


def reference(labeled, candidates, factor_rows, block_inverse):
    kernel_scale = 0.5 / math.sqrt(F)
    flat_rows = labeled.reshape(NB * B, F)
    kernel = jnp.exp(jnp.dot(flat_rows, candidates.T, preferred_element_type=jnp.float32) * kernel_scale)
    solved = []
    for number in range(NB):
        residual = kernel[number * B:(number + 1) * B]
        if number > 0:
            earlier = jnp.concatenate(solved, axis=0)
            residual = residual - jnp.dot(factor_rows[number][:, :number * B], earlier, preferred_element_type=jnp.float32)
        residual = residual.astype(jnp.bfloat16)
        solved.append(jnp.dot(block_inverse[number], residual, preferred_element_type=jnp.float32).astype(jnp.bfloat16))
    whitened = jnp.stack(solved, axis=0)
    explained = lax.optimization_barrier(jnp.sum(jnp.square(whitened.astype(jnp.float32)), axis=(0, 1)))
    return (whitened, explained)
```

```python
import functools
import math

import jax
import jax.numpy as jnp
from jax import lax
from jax.experimental import pallas as pl
from jax.experimental.pallas import tpu as pltpu
from jax.sharding import PartitionSpec as P

MESH = pl.DeviceIdType.MESH
BF = jnp.bfloat16
NX, NY, NZ = 4, 4, 8
QUARTER = 256
COLS = 128


def dot(a, b):
    return jnp.dot(a, b, preferred_element_type=jnp.float32)


def kernel(
    scale,
    lab,
    cand,
    fac,
    inv,
    out,
    expl,
    lbuf,
    cbuf,
    ibuf,
    fbuf0,
    fbuf1,
    fbuf2,
    kbuf,
    rbuf,
    wbuf,
    obuf,
    epart,
    esum,
    l1s,
    l1r,
    l2s,
    l2r,
    l3s,
    l3r,
    cs,
    cr,
    i1s,
    i1r,
    i2s,
    i2r,
    i3s,
    i3r,
    f1s,
    f1r,
    f2s,
    f2r,
    f3s,
    f3r,
    rs,
    rr,
    os,
    orr,
    es,
    er,
):
    g = lax.axis_index("grp")
    r = lax.axis_index("row")
    y, c = g // 2, g % 2
    x, z = r // NZ, r % NZ
    fbufs = (fbuf0, fbuf1, fbuf2)
    groups = ((0, 1), (1, 4))

    def x_peer(d):
        return (g, ((x + d) % NX) * NZ + z)

    def y_peer(d):
        return (((y + d) % NY) * 2 + c, r)

    def z_peer(d):
        return (g, x * NZ + (z + d) % NZ)

    core_peer = (y * 2 + 1 - c, r)

    def send(src, dst, ssem, rsem, device):
        pltpu.make_async_remote_copy(
            src_ref=src,
            dst_ref=dst,
            send_sem=ssem,
            recv_sem=rsem,
            device_id=device,
            device_id_type=MESH,
        ).start()

    def local(src, dst, sem):
        pltpu.make_async_copy(src, dst, sem).start()

    def await_bytes(ref, sem):
        pltpu.make_async_copy(ref, ref, sem).wait()

    def each_z(body):
        def step(d, carry):
            body(z_peer(d))
            return carry

        lax.fori_loop(1, NZ, step, 0)

    def rows_of(position):
        return pl.ds(pl.multiple_of(position * 32, 32), 32)

    own_rows = rows_of(z)

    def lab_z(k):
        lo, hi = groups[k]
        dst = lbuf.at[c, y, lo:hi, own_rows, :]
        local(lab.at[lo:hi], dst, l1r.at[k])
        each_z(lambda peer: send(lab.at[lo:hi], dst, l1s.at[k], l1r.at[k], peer))

    def lab_y(k):
        lo, hi = groups[k]
        await_bytes(lbuf.at[c, y, lo:hi], l1r.at[k])
        for d in range(1, NY):
            block = lbuf.at[c, y, lo:hi]
            send(block, block, l2s.at[k], l2r.at[k], y_peer(d))

    def lab_core(k):
        lo, hi = groups[k]
        await_bytes(lbuf.at[c, 0:3, lo:hi], l2r.at[k])
        block = lbuf.at[c, :, lo:hi]
        send(block, block, l3s.at[k], l3r.at[k], core_peer)

    def lab_wait(k):
        lo, hi = groups[k]
        await_bytes(lbuf.at[1 - c, :, lo:hi], l3r.at[k])

    def by_x(body):
        for number in range(NX):
            pl.when(x == number)(functools.partial(body, number))

    def inv_part(b, number, core):
        return ibuf.at[b, number, :, core, :, : (number + 1) * QUARTER]

    def inv_z(b):
        def go(number):
            width = (number + 1) * QUARTER
            src = inv.at[b, pl.ds(pl.multiple_of(c * 16, 16), 16), :width]
            dst = ibuf.at[b, number, z, c, :, :width]
            local(src, dst, i1r.at[b])
            each_z(lambda peer: send(src, dst, i1s.at[b], i1r.at[b], peer))

        by_x(go)

    def inv_x(b):
        def go(number):
            part = inv_part(b, number, c)
            await_bytes(part, i1r.at[b])
            if b < 3:
                for d in range(1, NX):
                    send(part, part, i2s.at[b], i2r.at[b, number], x_peer(d))
            send(part, part, i3s.at[b], i3r.at[b, number], core_peer)

        by_x(go)

    def inv_core(b):
        for number in range(NX):

            @pl.when(x != number)
            def _():
                part = inv_part(b, number, c)
                await_bytes(part, i2r.at[b, number])
                send(part, part, i3s.at[b], i3r.at[b, number], core_peer)

    def inv_wait(b):
        if b < 3:
            for number in range(NX):
                await_bytes(inv_part(b, number, 1 - c), i3r.at[b, number])
        else:
            by_x(lambda number: await_bytes(inv_part(b, number, 1 - c), i3r.at[b, number]))

    def fac_z(j):
        src = fac.at[j + 1 : 4, :, pl.ds(pl.multiple_of(j * 1024 + g * 128, 128), 128)]
        dst = fbufs[j].at[c, y, :, own_rows, :]
        local(src, dst, f1r.at[j])
        each_z(lambda peer: send(src, dst, f1s.at[j], f1r.at[j], peer))

    def fac_y(j):
        block = fbufs[j].at[c, y]
        await_bytes(block, f1r.at[j])
        for d in range(1, NY):
            send(block, block, f2s.at[j], f2r.at[j], y_peer(d))

    def fac_core(j):
        await_bytes(fbufs[j].at[c, 0:3], f2r.at[j])
        half = fbufs[j].at[c]
        send(half, half, f3s.at[j], f3r.at[j], core_peer)

    def fac_wait(j):
        await_bytes(fbufs[j].at[1 - c], f3r.at[j])

    def make_kernel(b):
        rows = jnp.concatenate([lbuf[k % 2, k // 2, b] for k in range(8)], axis=1)
        sums = lax.dot_general(
            rows,
            cbuf[...].reshape(COLS, 1024),
            (((1,), (1,)), ((), ())),
            preferred_element_type=jnp.float32,
        )
        kbuf[b] = jnp.exp(sums * scale)

    def publish(b):
        rbuf[b, x] = kbuf[b].astype(BF)
        for d in range(1, NX):
            send(rbuf.at[b, x], rbuf.at[b, x], rs.at[b], rr.at[b], x_peer(d))

    def residual_wait(b):
        await_bytes(rbuf.at[b, 0:3], rr.at[b])

    def solve(b):
        residual = rbuf[b].reshape(1024, COLS)

        def rows(number):
            width = (number + 1) * QUARTER
            left = ibuf[b, number, :, :, :, :width].reshape(QUARTER, width)
            wbuf[b, number] = dot(left, residual[:width]).astype(BF)

        if b < 3:
            for number in range(NX):
                rows(number)
        else:
            by_x(rows)

    def spread(b):
        dst = obuf.at[z, b]
        local(wbuf.at[b, x, own_rows, :], dst, orr.at[b])

        def step(d, carry):
            other = (z + d) % NZ
            send(
                wbuf.at[b, x, rows_of(other), :],
                dst,
                os.at[b],
                orr.at[b],
                (g, x * NZ + other),
            )
            return carry

        lax.fori_loop(1, NZ, step, 0)

    def update(j, b):
        panel = jnp.concatenate(
            [fbufs[j][k % 2, k // 2, b - j - 1] for k in range(8)], axis=1
        )
        kbuf[b] = kbuf[b] - dot(panel, wbuf[j].reshape(1024, COLS))

    barrier = pltpu.get_barrier_semaphore()
    peers = [x_peer(d) for d in range(1, NX)] + [y_peer(d) for d in range(1, NY)]
    peers += [z_peer(d) for d in range(1, NZ)] + [core_peer]
    for peer in peers:
        pl.semaphore_signal(barrier, inc=1, device_id=peer, device_id_type=MESH)
    pl.semaphore_wait(barrier, len(peers))

    lab_z(0)
    local(cand, cbuf.at[x], cr)
    for d in range(1, NX):
        send(cand, cbuf.at[x], cs, cr, x_peer(d))
    inv_z(0)
    lab_z(1)
    fac_z(0)
    lab_y(0)
    inv_z(1)
    inv_x(0)
    fac_z(1)
    inv_z(2)
    fac_z(2)
    inv_z(3)
    lab_core(0)
    lab_y(1)
    await_bytes(cbuf, cr)
    lab_wait(0)
    make_kernel(0)
    publish(0)
    fac_y(0)
    inv_core(0)
    inv_x(1)
    lab_core(1)
    inv_wait(0)
    residual_wait(0)
    solve(0)
    spread(0)
    fac_core(0)
    lab_wait(1)
    for b in range(1, 4):
        make_kernel(b)
    fac_wait(0)
    update(0, 1)
    publish(1)
    inv_core(1)
    fac_y(1)
    inv_x(2)
    update(0, 2)
    update(0, 3)
    inv_wait(1)
    residual_wait(1)
    solve(1)
    spread(1)
    fac_core(1)
    fac_wait(1)
    update(1, 2)
    publish(2)
    inv_core(2)
    fac_y(2)
    inv_x(3)
    update(1, 3)
    inv_wait(2)
    residual_wait(2)
    solve(2)
    spread(2)
    fac_core(2)
    fac_wait(2)
    update(2, 3)
    publish(3)

    for k, (lo, hi) in enumerate(groups):
        await_bytes(lbuf.at[c, y, lo:hi, 0:224, :], l1s.at[k])
        await_bytes(lbuf.at[c, 0:3, lo:hi], l2s.at[k])
        await_bytes(lbuf.at[c, :, lo:hi], l3s.at[k])
    await_bytes(cbuf.at[0:3], cs)
    for j in range(3):
        await_bytes(fbufs[j].at[c, y, :, 0:224, :], f1s.at[j])
        await_bytes(fbufs[j].at[c, 0:3], f2s.at[j])
        await_bytes(fbufs[j].at[c], f3s.at[j])

    def owed(number):
        for b in range(4):
            part = inv_part(b, number, c)
            await_bytes(ibuf.at[b, number, 0:7, c, :, : (number + 1) * QUARTER], i1s.at[b])
            if b < 3:
                for _ in range(1, NX):
                    await_bytes(part, i2s.at[b])

    by_x(owed)
    for b in range(3):
        for number in range(NX):
            await_bytes(inv_part(b, number, c), i3s.at[b])
    by_x(lambda number: await_bytes(inv_part(3, number, c), i3s.at[3]))
    inv_wait(3)
    residual_wait(3)
    solve(3)
    spread(3)

    total = jnp.zeros((1, COLS), jnp.float32)
    for b in range(4):
        values = wbuf[b, x].astype(jnp.float32)
        total = total + jnp.sum(values * values, axis=0, keepdims=True)
    epart[x] = total
    for d in range(1, NX):
        send(epart.at[x], epart.at[x], es.at[0], er.at[0], x_peer(d))
    await_bytes(epart.at[0:3], er.at[0])
    esum[z] = epart[0] + epart[1] + epart[2] + epart[3]
    each_z(lambda peer: send(esum.at[z], esum.at[z], es.at[1], er.at[1], peer))

    source = lax.broadcasted_iota(jnp.int32, (512, 128), 0)
    target = lax.broadcasted_iota(jnp.int32, (512, 128), 1)
    pickers = []
    for chunk in range(NX):
        wanted = (target // 32) * 128 + chunk * 32 + target % 32
        pickers.append(jnp.where(source == wanted, 1.0, 0.0).astype(BF))
    for b in range(4):
        await_bytes(obuf.at[:, b], orr.at[b])
    for half in range(2):
        rows = jnp.concatenate(
            [obuf[half * 4 + k].reshape(128, COLS) for k in range(4)], axis=1
        )
        for chunk in range(NX):
            tile = dot(rows, pickers[chunk]).astype(BF)
            tile = tile.reshape(4, 32, COLS)
            at = (chunk * 2 + half) * 128
            for b in range(4):
                out[b, :, at : at + 128] = tile[b]

    await_bytes(esum.at[0:7], er.at[1])
    lane = lax.broadcasted_iota(jnp.int32, (1, 128), 1) // 32
    for chunk in range(NX):
        for half in range(2):
            row = jnp.zeros((1, COLS), jnp.float32)
            for k in range(4):
                moved = pltpu.roll(esum[half * 4 + k], ((k - chunk) % 4) * 32, 1)
                row = jnp.where(lane == k, moved, row)
            expl[chunk * 2 + half : chunk * 2 + half + 1, :] = row

    for b in range(4):
        await_bytes(rbuf.at[b, 0:3], rs.at[b])
        await_bytes(obuf.at[0:7, b], os.at[b])
    await_bytes(epart.at[0:3], es.at[0])
    await_bytes(esum.at[0:7], es.at[1])


def on_device(labeled, candidates, factor_rows, block_inverse):
    dma = pltpu.SemaphoreType.DMA
    scale = 0.5 / math.sqrt(1024)
    whitened, explained = pl.pallas_call(
        functools.partial(kernel, scale),
        out_shape=(
            jax.ShapeDtypeStruct((4, 32, 1024), BF),
            jax.ShapeDtypeStruct((8, 128), jnp.float32),
        ),
        in_specs=[pl.BlockSpec(memory_space=pl.ANY)] * 4,
        out_specs=(
            pl.BlockSpec(memory_space=pltpu.VMEM),
            pl.BlockSpec(memory_space=pltpu.VMEM),
        ),
        scratch_shapes=[
            pltpu.VMEM((2, NY, 4, QUARTER, 128), BF),
            pltpu.VMEM((NX, 32, 1024), BF),
            pltpu.VMEM((4, NX, NZ, 2, 16, 1024), BF),
            pltpu.VMEM((2, NY, 3, QUARTER, 128), BF),
            pltpu.VMEM((2, NY, 2, QUARTER, 128), BF),
            pltpu.VMEM((2, NY, 1, QUARTER, 128), BF),
            pltpu.VMEM((4, QUARTER, COLS), jnp.float32),
            pltpu.VMEM((4, NX, QUARTER, COLS), BF),
            pltpu.VMEM((4, NX, QUARTER, COLS), BF),
            pltpu.VMEM((NZ, 4, 32, COLS), BF),
            pltpu.VMEM((NX, 1, COLS), jnp.float32),
            pltpu.VMEM((NZ, 1, COLS), jnp.float32),
            dma((2,)),
            dma((2,)),
            dma((2,)),
            dma((2,)),
            dma((2,)),
            dma((2,)),
            dma,
            dma,
            dma((4,)),
            dma((4,)),
            dma((3,)),
            dma((3, NX)),
            dma((4,)),
            dma((4, NX)),
            dma((3,)),
            dma((3,)),
            dma((3,)),
            dma((3,)),
            dma((3,)),
            dma((3,)),
            dma((4,)),
            dma((4,)),
            dma((4,)),
            dma((4,)),
            dma((2,)),
            dma((2,)),
        ],
        compiler_params=pltpu.CompilerParams(
            collective_id=0, has_side_effects=True, vmem_limit_bytes=40 * 1024 * 1024
        ),
        name="whiten",
    )(labeled, candidates, factor_rows, block_inverse)
    return whitened, explained.reshape(1024)


def solution(mesh):
    in_specs = (
        P(None, "row", "grp"),
        P(("grp", "row"), None),
        P(None, "row", None),
        P(None, "row", None),
    )
    out_specs = (P(None, "row", "grp"), P("grp"))
    return jax.shard_map(
        on_device, mesh=mesh, in_specs=in_specs, out_specs=out_specs, check_vma=False
    )
```

```python
import functools
import math

import jax
import jax.numpy as jnp
from jax import lax
from jax.experimental import pallas as pl
from jax.experimental.pallas import tpu as pltpu
from jax.sharding import PartitionSpec as P

MESH = pl.DeviceIdType.MESH
BF = jnp.bfloat16
NX, NY, NZ = 4, 4, 8
QUARTER = 256
COLS = 128
VMEM_BYTES = 63 * 1024 * 1024
ITEMS = [("inv", 0), ("inv", 1), ("inv", 2), ("inv", 3)]
ITEMS += [("row", 0), ("row", 1), ("row", 2), ("row", 3)]
FULL = (True, False, False, False)
Y_STEPS = ((1, 3, 2), (1, 3, 2), (1, 3, 2), (1, 3, 2))
X_STEPS = ((1, 3, 2), (1, 3), (1, 3))


def dot(a, b):
    return jnp.dot(a, b, preferred_element_type=jnp.float32)


def kernel(
    scale,
    lab,
    cand,
    fac,
    inv,
    out,
    expl,
    mbuf0,
    mbuf1,
    mbuf2,
    mbuf3,
    cbuf,
    ibuf,
    kbuf,
    rbuf,
    wbuf,
    obuf,
    pick,
    epart,
    esum,
    own_sem,
    zs,
    zr,
    m1s,
    m1r,
    m2s,
    m2r,
    m3s,
    m3r,
    cs,
    cr,
    i2s,
    i2r,
    i3s,
    i3r,
    rs,
    rr,
    ws,
    wr,
    os,
    orr,
    es,
    er,
):
    g = lax.axis_index("grp")
    r = lax.axis_index("row")
    y, c = g // 2, g % 2
    x, z = r // NZ, r % NZ
    mbufs = (mbuf0, mbuf1, mbuf2, mbuf3)

    def x_peer(d):
        return (g, ((x + d) % NX) * NZ + z)

    def y_peer(d):
        return (((y + d) % NY) * 2 + c, r)

    def z_peer(d):
        return (g, x * NZ + (z + d) % NZ)

    core_peer = (y * 2 + 1 - c, r)

    def send(src, dst, ssem, rsem, device):
        pltpu.make_async_remote_copy(
            src_ref=src,
            dst_ref=dst,
            send_sem=ssem,
            recv_sem=rsem,
            device_id=device,
            device_id_type=MESH,
        ).start()

    def local(src, dst, sem):
        pltpu.make_async_copy(src, dst, sem).start()

    def await_bytes(ref, sem):
        pltpu.make_async_copy(ref, ref, sem).wait()

    def each_z(body):
        def step(d, carry):
            body(z_peer(d))
            return carry

        lax.fori_loop(1, NZ, step, 0)

    def rows_of(position):
        return pl.ds(pl.multiple_of(position * 32, 32), 32)

    own_rows = rows_of(z)

    side = 1 - 2 * c

    def along(distance):
        return (z + NZ + distance) % NZ

    def z_at(distance):
        return (g, x * NZ + along(distance))

    def slots(item, first, count):
        rows = pl.ds(pl.multiple_of(first * 32, 32), count * 32)
        return mbufs[item[1]].at[c, y, :, rows, :]

    def inv_slots(b, number, first, count):
        width = (number + 1) * QUARTER
        return ibuf.at[b, number, pl.ds(first, count), c, :, :width]

    def at_slots(item, body):
        if item[0] == "inv":
            by_x(lambda number: body(functools.partial(inv_slots, item[1], number)))
        else:
            body(functools.partial(slots, item))

    def by_x(body):
        for number in range(NX):
            pl.when(x == number)(functools.partial(body, number))

    def begin(item):
        n = ITEMS.index(item)

        def go(at):
            own = at(z, 1)
            await_bytes(own, own_sem.at[n])
            for distance in (2, -2, 1, -1):
                near = 0 if abs(distance) == 2 else 1
                send(own, own, zs.at[n], zr.at[n, near], z_at(distance))

        at_slots(item, go)

    def relay(item):
        n = ITEMS.index(item)

        def go(at):
            await_bytes(at(0, 2), zr.at[n, 0])
            for distance in (2, -2):
                one = at(along(-distance), 1)
                send(one, one, zs.at[n], zr.at[n, 2], z_at(distance // 2))
            far = at(along(-2 * side), 1)
            send(far, far, zs.at[n], zr.at[n, 2], z_at(2 * side))

        at_slots(item, go)

    def arrive(item):
        n = ITEMS.index(item)

        def go(at):
            await_bytes(at(0, 2), zr.at[n, 1])
            await_bytes(at(0, 3), zr.at[n, 2])

        at_slots(item, go)

    def row_first():
        own = slots(("row", 0), z, 1)
        await_bytes(own, own_sem.at[ITEMS.index(("row", 0))])
        each_z(lambda peer: send(own, own, m1s, m1r, peer))

    def row_y(b):
        block = mbufs[b].at[c, y]
        if b == 0:
            await_bytes(mbuf0.at[c, y, :, 0:224, :], m1r)
        else:
            arrive(("row", b))
        for d in Y_STEPS[b]:
            send(block, block, m2s.at[b], m2r.at[b, d], y_peer(d))

    def row_relay(b, step):
        lo = 0 if step == 1 else 128
        other = (y + NY - step) % NY
        await_bytes(mbufs[b].at[c, other], m2r.at[b, step])
        if len(Y_STEPS[b]) == 2:
            half = mbufs[b].at[c, other, :, lo : lo + 128, :]
            send(half, half, m2s.at[b], m2r.at[b, 2], y_peer(step))

    def row_core(b):
        await_bytes(mbufs[b].at[c, 0], m2r.at[b, 2])
        half = mbufs[b].at[c]
        send(half, half, m3s.at[b], m3r.at[b], core_peer)

    def row_wait(b):
        await_bytes(mbufs[b].at[1 - c], m3r.at[b])

    def inv_part(b, number, core, lo=0, hi=NZ):
        return ibuf.at[b, number, lo:hi, core, :, : (number + 1) * QUARTER]

    def inv_across(b, number):
        part = inv_part(b, number, c)
        send(part, part, i3s.at[b], i3r.at[b, number], core_peer)

    def inv_x(b):
        arrive(("inv", b))

        def go(number):
            part = inv_part(b, number, c)
            if FULL[b]:
                for d in X_STEPS[b]:
                    send(part, part, i2s.at[b], i2r.at[b, number], x_peer(d))
            inv_across(b, number)

        by_x(go)

    def inv_relay(b, step):
        lo = 0 if step == 1 else 4

        def go(number):
            other = (number + NX - step) % NX
            await_bytes(inv_part(b, other, c), i2r.at[b, other])
            if len(X_STEPS[b]) == 2:
                half = inv_part(b, other, c, lo, lo + 4)
                send(half, half, i2s.at[b], i2r.at[b, other], x_peer(step))
            inv_across(b, other)

        by_x(go)

    def inv_core(b):
        def go(number):
            far = (number + 2) % NX
            await_bytes(inv_part(b, far, c), i2r.at[b, far])
            inv_across(b, far)

        by_x(go)

    def inv_wait(b):
        if FULL[b]:
            for number in range(NX):
                await_bytes(inv_part(b, number, 1 - c), i3r.at[b, number])
        else:
            by_x(lambda number: await_bytes(inv_part(b, number, 1 - c), i3r.at[b, number]))

    def make_kernel(b):
        rows = jnp.concatenate([mbufs[b][k % 2, k // 2, 0] for k in range(8)], axis=1)
        sums = lax.dot_general(
            rows,
            cbuf[...].reshape(COLS, 1024),
            (((1,), (1,)), ((), ())),
            preferred_element_type=jnp.float32,
        )
        kbuf[b] = jnp.exp(sums * scale)

    def publish(b):
        rbuf[b, x] = kbuf[b].astype(BF)
        for d in range(1, NX):
            send(rbuf.at[b, x], rbuf.at[b, x], rs.at[b], rr.at[b], x_peer(d))

    def residual_wait(b):
        await_bytes(rbuf.at[b, 0:3], rr.at[b])

    def solve(b):
        residual = rbuf[b].reshape(1024, COLS)

        def rows(number):
            width = (number + 1) * QUARTER
            left = ibuf[b, number, :, :, :, :width].reshape(QUARTER, width)
            wbuf[b, number] = dot(left, residual[:width]).astype(BF)

        if FULL[b]:
            for number in range(NX):
                rows(number)
        else:
            by_x(rows)

    def share(b):
        for d in range(1, NX):
            send(wbuf.at[b, x], wbuf.at[b, x], ws.at[b], wr.at[b], x_peer(d))

    def share_wait(b):
        await_bytes(wbuf.at[b, 0:3], wr.at[b])

    def spread(b):
        dst = obuf.at[z, b]
        local(wbuf.at[b, x, own_rows, :], dst, orr.at[b])

        def step(d, carry):
            other = (z + d) % NZ
            send(
                wbuf.at[b, x, rows_of(other), :],
                dst,
                os.at[b],
                orr.at[b],
                (g, x * NZ + other),
            )
            return carry

        lax.fori_loop(1, NZ, step, 0)

    def update(j, b):
        parts = [mbufs[b][k % 2, k // 2, j + 1] for k in range(8)]
        panel = jnp.concatenate(parts, axis=1)
        kbuf[b] = kbuf[b] - dot(panel, wbuf[j].reshape(1024, COLS))

    def make_pickers():
        source = lax.broadcasted_iota(jnp.int32, (512, 128), 0)
        target = lax.broadcasted_iota(jnp.int32, (512, 128), 1)
        for chunk in range(NX):
            wanted = (target // 32) * 128 + chunk * 32 + target % 32
            pick[chunk] = jnp.where(source == wanted, 1.0, 0.0).astype(BF)

    def assemble(b):
        await_bytes(obuf.at[:, b], orr.at[b])
        for half in range(2):
            rows = jnp.concatenate([obuf[half * 4 + k, b] for k in range(4)], axis=1)
            for chunk in range(NX):
                at = (chunk * 2 + half) * 128
                out[b, :, at : at + 128] = dot(rows, pick[chunk]).astype(BF)

    barrier = pltpu.get_barrier_semaphore()
    peers = [x_peer(d) for d in range(1, NX)] + [y_peer(d) for d in range(1, NY)]
    peers += [z_peer(d) for d in range(1, NZ)] + [core_peer]
    for peer in peers:
        pl.semaphore_signal(barrier, inc=1, device_id=peer, device_id_type=MESH)
    def own_inv(b):
        def go(number):
            width = (number + 1) * QUARTER
            half = pl.ds(pl.multiple_of(c * 16, 16), 16)
            local(inv.at[b, half, :width], ibuf.at[b, number, z, c, :, :width], own_sem.at[b])

        by_x(go)

    def own_row(b):
        sem = own_sem.at[4 + b]
        local(lab.at[b], mbufs[b].at[c, y, 0, own_rows, :], sem)
        for j in range(b):
            cols = pl.ds(pl.multiple_of(j * 1024 + g * 128, 128), 128)
            local(fac.at[b, :, cols], mbufs[b].at[c, y, j + 1, own_rows, :], sem)

    own_row(0)
    local(cand, cbuf.at[x], own_sem.at[8])
    for b in range(4):
        own_inv(b)
        if b < 3:
            own_row(b + 1)
    pl.semaphore_wait(barrier, len(peers))

    i0, i1, i2, i3 = [("inv", b) for b in range(4)]
    m1, m2, m3 = [("row", b) for b in range(1, 4)]
    make_pickers()

    row_first()
    await_bytes(cbuf.at[x], own_sem.at[8])
    for d in range(1, NX):
        send(cbuf.at[x], cbuf.at[x], cs, cr, x_peer(d))
    begin(i0)
    begin(m1)
    begin(i1)
    relay(i0)
    relay(m1)
    row_y(0)
    begin(m2)
    inv_x(0)
    row_y(1)
    relay(i1)
    begin(i2)
    row_relay(0, 1)
    row_relay(0, 3)
    row_core(0)
    await_bytes(cbuf.at[0:3], cr)
    relay(m2)
    row_wait(0)
    make_kernel(0)
    publish(0)
    begin(m3)
    relay(i2)
    inv_x(1)
    begin(i3)
    row_relay(1, 1)
    row_relay(1, 3)
    row_core(1)
    row_y(2)
    inv_relay(0, 1)
    inv_relay(0, 3)
    inv_core(0)
    relay(m3)
    relay(i3)
    row_wait(1)
    make_kernel(1)
    inv_wait(0)
    residual_wait(0)
    solve(0)
    spread(0)
    update(0, 1)
    publish(1)
    inv_x(2)
    row_relay(2, 1)
    row_relay(2, 3)
    row_y(3)
    row_core(2)
    row_wait(2)
    make_kernel(2)
    update(0, 2)
    inv_wait(1)
    residual_wait(1)
    solve(1)
    share(1)
    spread(1)
    share_wait(1)
    update(1, 2)
    publish(2)
    row_relay(3, 1)
    row_relay(3, 3)
    inv_x(3)
    row_core(3)
    row_wait(3)
    make_kernel(3)
    update(0, 3)
    update(1, 3)
    inv_wait(2)
    residual_wait(2)
    solve(2)
    share(2)
    spread(2)
    share_wait(2)
    update(2, 3)
    publish(3)

    for b in range(3):
        assemble(b)
    await_bytes(mbuf0.at[c, y, :, 0:224, :], m1s)
    for b in range(4):
        if b > 0:
            await_bytes(mbufs[b].at[c, y, :, 0:224, :], zs.at[ITEMS.index(("row", b))])
        await_bytes(mbufs[b].at[c, 0:3], m2s.at[b])
        await_bytes(mbufs[b].at[c], m3s.at[b])
    await_bytes(cbuf.at[0:3], cs)
    def owed(number):
        for b in range(4):
            await_bytes(inv_part(b, number, c, 0, 7), zs.at[ITEMS.index(("inv", b))])
            if FULL[b]:
                for _ in X_STEPS[b]:
                    await_bytes(inv_part(b, number, c), i2s.at[b])
                if len(X_STEPS[b]) == 2:
                    await_bytes(inv_part(b, (number - 1) % NX, c, 0, 4), i2s.at[b])
                    await_bytes(inv_part(b, (number + 1) % NX, c, 4, 8), i2s.at[b])

    by_x(owed)
    for b in range(4):
        if FULL[b]:
            for number in range(NX):
                await_bytes(inv_part(b, number, c), i3s.at[b])
        else:
            by_x(lambda number: await_bytes(inv_part(b, number, c), i3s.at[b]))
            if b < 3:
                await_bytes(wbuf.at[b, 0:3], ws.at[b])
    inv_wait(3)
    residual_wait(3)
    solve(3)
    spread(3)

    total = jnp.zeros((1, COLS), jnp.float32)
    for b in range(4):
        values = wbuf[b, x].astype(jnp.float32)
        total = total + jnp.sum(values * values, axis=0, keepdims=True)
    epart[x] = total
    for d in range(1, NX):
        send(epart.at[x], epart.at[x], es.at[0], er.at[0], x_peer(d))
    await_bytes(epart.at[0:3], er.at[0])
    esum[z] = epart[0] + epart[1] + epart[2] + epart[3]
    each_z(lambda peer: send(esum.at[z], esum.at[z], es.at[1], er.at[1], peer))

    assemble(3)

    await_bytes(esum.at[0:7], er.at[1])
    lane = lax.broadcasted_iota(jnp.int32, (1, 128), 1) // 32
    for chunk in range(NX):
        for half in range(2):
            row = jnp.zeros((1, COLS), jnp.float32)
            for k in range(4):
                moved = pltpu.roll(esum[half * 4 + k], ((k - chunk) % 4) * 32, 1)
                row = jnp.where(lane == k, moved, row)
            expl[chunk * 2 + half : chunk * 2 + half + 1, :] = row

    for b in range(4):
        await_bytes(rbuf.at[b, 0:3], rs.at[b])
        await_bytes(obuf.at[0:7, b], os.at[b])
    await_bytes(epart.at[0:3], es.at[0])
    await_bytes(esum.at[0:7], es.at[1])


def on_device(labeled, candidates, factor_rows, block_inverse):
    dma = pltpu.SemaphoreType.DMA
    scale = 0.5 / math.sqrt(1024)
    whitened, explained = pl.pallas_call(
        functools.partial(kernel, scale),
        out_shape=(
            jax.ShapeDtypeStruct((4, 32, 1024), BF),
            jax.ShapeDtypeStruct((8, 128), jnp.float32),
        ),
        in_specs=[pl.BlockSpec(memory_space=pltpu.HBM)] * 4,
        out_specs=(
            pl.BlockSpec(memory_space=pltpu.VMEM),
            pl.BlockSpec(memory_space=pltpu.VMEM),
        ),
        scratch_shapes=[
            pltpu.VMEM((2, NY, 1, QUARTER, 128), BF),
            pltpu.VMEM((2, NY, 2, QUARTER, 128), BF),
            pltpu.VMEM((2, NY, 3, QUARTER, 128), BF),
            pltpu.VMEM((2, NY, 4, QUARTER, 128), BF),
            pltpu.VMEM((NX, 32, 1024), BF),
            pltpu.VMEM((4, NX, NZ, 2, 16, 1024), BF),
            pltpu.VMEM((4, QUARTER, COLS), jnp.float32),
            pltpu.VMEM((4, NX, QUARTER, COLS), BF),
            pltpu.VMEM((4, NX, QUARTER, COLS), BF),
            pltpu.VMEM((NZ, 4, 32, COLS), BF),
            pltpu.VMEM((NX, 512, 128), BF),
            pltpu.VMEM((NX, 1, COLS), jnp.float32),
            pltpu.VMEM((NZ, 1, COLS), jnp.float32),
            dma((9,)),
            dma((8,)),
            dma((8, 3)),
            dma,
            dma,
            dma((4,)),
            dma((4, NY)),
            dma((4,)),
            dma((4,)),
            dma,
            dma,
            dma((3,)),
            dma((3, NX)),
            dma((4,)),
            dma((4, NX)),
            dma((4,)),
            dma((4,)),
            dma((3,)),
            dma((3,)),
            dma((4,)),
            dma((4,)),
            dma((2,)),
            dma((2,)),
        ],
        compiler_params=pltpu.CompilerParams(
            collective_id=0, has_side_effects=True, vmem_limit_bytes=VMEM_BYTES
        ),
        name="whiten",
    )(labeled, candidates, factor_rows, block_inverse)
    return whitened, explained.reshape(1024)


def solution(mesh):
    in_specs = (
        P(None, "row", "grp"),
        P(("grp", "row"), None),
        P(None, "row", None),
        P(None, "row", None),
    )
    out_specs = (P(None, "row", "grp"), P("grp"))
    return jax.shard_map(
        on_device, mesh=mesh, in_specs=in_specs, out_specs=out_specs, check_vma=False
    )
```

```python
import functools
import math

import jax
import jax.numpy as jnp
from jax import lax
from jax.experimental import pallas as pl
from jax.experimental.pallas import tpu as pltpu
from jax.sharding import PartitionSpec as P

MESH = pl.DeviceIdType.MESH
BF = jnp.bfloat16
NX, NY, NZ = 4, 4, 8
QUARTER = 256
COLS = 128
VMEM_BYTES = 63 * 1024 * 1024
ITEMS = [("inv", 0), ("inv", 1), ("inv", 2), ("inv", 3)]
ITEMS += [("row", 0), ("row", 1), ("row", 2), ("row", 3)]
Z_DIRECT = ()
FULL = (True, False, False, False)
Y_STEPS = ((1, 3, 2), (1, 3, 2), (1, 3, 2), (1, 3, 2))
X_STEPS = ((1, 3), (1, 3), (1, 3))


def dot(a, b):
    return jnp.dot(a, b, preferred_element_type=jnp.float32)


def kernel(
    scale,
    lab,
    cand,
    fac,
    inv,
    out,
    expl,
    mbuf0,
    mbuf1,
    mbuf2,
    mbuf3,
    cbuf,
    ibuf,
    kbuf,
    rbuf,
    wbuf,
    obuf,
    pick,
    epart,
    own_sem,
    zs,
    zr,
    m1s,
    m1r,
    m2s,
    m2r,
    m3s,
    m3r,
    cs,
    cr,
    i2s,
    i2r,
    i3s,
    i3r,
    rs,
    rr,
    ws,
    wr,
    os,
    orr,
    es,
    er,
):
    g = lax.axis_index("grp")
    r = lax.axis_index("row")
    y, c = g // 2, g % 2
    x, z = r // NZ, r % NZ
    mbufs = (mbuf0, mbuf1, mbuf2, mbuf3)

    def x_peer(d):
        return (g, ((x + d) % NX) * NZ + z)

    def y_peer(d):
        return (((y + d) % NY) * 2 + c, r)

    def z_peer(d):
        return (g, x * NZ + (z + d) % NZ)

    core_peer = (y * 2 + 1 - c, r)

    def send(src, dst, ssem, rsem, device):
        pltpu.make_async_remote_copy(
            src_ref=src,
            dst_ref=dst,
            send_sem=ssem,
            recv_sem=rsem,
            device_id=device,
            device_id_type=MESH,
        ).start()

    def local(src, dst, sem):
        pltpu.make_async_copy(src, dst, sem).start()

    def await_bytes(ref, sem):
        pltpu.make_async_copy(ref, ref, sem).wait()

    def each_z(body):
        def step(d, carry):
            body(z_peer(d))
            return carry

        lax.fori_loop(1, NZ, step, 0)

    def rows_of(position):
        return pl.ds(pl.multiple_of(position * 32, 32), 32)

    own_rows = rows_of(z)

    side = 1 - 2 * c

    def along(distance):
        return (z + NZ + distance) % NZ

    def z_at(distance):
        return (g, x * NZ + along(distance))

    def slots(item, first, count):
        rows = pl.ds(pl.multiple_of(first * 32, 32), count * 32)
        return mbufs[item[1]].at[c, y, :, rows, :]

    def inv_slots(b, number, first, count):
        width = (number + 1) * QUARTER
        return ibuf.at[b, number, pl.ds(first, count), c, :, :width]

    def at_slots(item, body):
        if item[0] == "inv":
            by_x(lambda number: body(functools.partial(inv_slots, item[1], number)))
        else:
            body(functools.partial(slots, item))

    def by_x(body):
        for number in range(NX):
            pl.when(x == number)(functools.partial(body, number))

    def begin(item):
        n = ITEMS.index(item)

        def go(at):
            own = at(z, 1)
            await_bytes(own, own_sem.at[n])
            if item in Z_DIRECT:
                each_z(lambda peer: send(own, own, zs.at[n], zr.at[n, 0], peer))
                return
            for distance in (2, -2, 1, -1):
                near = 0 if abs(distance) == 2 else 1
                send(own, own, zs.at[n], zr.at[n, near], z_at(distance))

        at_slots(item, go)

    def relay(item):
        n = ITEMS.index(item)
        if item in Z_DIRECT:
            return

        def go(at):
            await_bytes(at(0, 2), zr.at[n, 0])
            for distance in (2, -2):
                one = at(along(-distance), 1)
                send(one, one, zs.at[n], zr.at[n, 2], z_at(distance // 2))
            far = at(along(-2 * side), 1)
            send(far, far, zs.at[n], zr.at[n, 2], z_at(2 * side))

        at_slots(item, go)

    def arrive(item):
        n = ITEMS.index(item)

        def go(at):
            if item in Z_DIRECT:
                await_bytes(at(0, 7), zr.at[n, 0])
                return
            await_bytes(at(0, 2), zr.at[n, 1])
            await_bytes(at(0, 3), zr.at[n, 2])

        at_slots(item, go)

    def row_first():
        own = slots(("row", 0), z, 1)
        await_bytes(own, own_sem.at[ITEMS.index(("row", 0))])
        each_z(lambda peer: send(own, own, m1s, m1r, peer))

    def row_y(b):
        block = mbufs[b].at[c, y]
        if b == 0:
            await_bytes(mbuf0.at[c, y, :, 0:224, :], m1r)
        else:
            arrive(("row", b))
        for d in Y_STEPS[b]:
            send(block, block, m2s.at[b], m2r.at[b, d], y_peer(d))

    def row_relay(b, step):
        lo = 0 if step == 1 else 128
        other = (y + NY - step) % NY
        await_bytes(mbufs[b].at[c, other], m2r.at[b, step])
        if len(Y_STEPS[b]) == 2:
            half = mbufs[b].at[c, other, :, lo : lo + 128, :]
            send(half, half, m2s.at[b], m2r.at[b, 2], y_peer(step))

    def row_core(b):
        await_bytes(mbufs[b].at[c, 0], m2r.at[b, 2])
        half = mbufs[b].at[c]
        send(half, half, m3s.at[b], m3r.at[b], core_peer)

    def row_wait(b):
        await_bytes(mbufs[b].at[1 - c], m3r.at[b])

    def inv_part(b, number, core, lo=0, hi=NZ):
        return ibuf.at[b, number, lo:hi, core, :, : (number + 1) * QUARTER]

    def inv_across(b, number):
        part = inv_part(b, number, c)
        send(part, part, i3s.at[b], i3r.at[b, number], core_peer)

    def inv_x(b):
        arrive(("inv", b))

        def go(number):
            part = inv_part(b, number, c)
            if FULL[b]:
                for d in X_STEPS[b]:
                    send(part, part, i2s.at[b], i2r.at[b, number], x_peer(d))
            inv_across(b, number)

        by_x(go)

    def inv_relay(b, step):
        lo = 0 if step == 1 else 4

        def go(number):
            other = (number + NX - step) % NX
            await_bytes(inv_part(b, other, c), i2r.at[b, other])
            if len(X_STEPS[b]) == 2:
                half = inv_part(b, other, c, lo, lo + 4)
                send(half, half, i2s.at[b], i2r.at[b, other], x_peer(step))
            inv_across(b, other)

        by_x(go)

    def inv_core(b):
        def go(number):
            far = (number + 2) % NX
            await_bytes(inv_part(b, far, c), i2r.at[b, far])
            inv_across(b, far)

        by_x(go)

    def inv_wait(b):
        if FULL[b]:
            for number in range(NX):
                await_bytes(inv_part(b, number, 1 - c), i3r.at[b, number])
        else:
            by_x(lambda number: await_bytes(inv_part(b, number, 1 - c), i3r.at[b, number]))

    def make_kernel(b):
        rows = jnp.concatenate([mbufs[b][k % 2, k // 2, 0] for k in range(8)], axis=1)
        sums = lax.dot_general(
            rows,
            cbuf[...].reshape(COLS, 1024),
            (((1,), (1,)), ((), ())),
            preferred_element_type=jnp.float32,
        )
        kbuf[b] = jnp.exp(sums * scale)

    def publish(b):
        rbuf[b, x] = kbuf[b].astype(BF)
        for d in range(1, NX):
            send(rbuf.at[b, x], rbuf.at[b, x], rs.at[b], rr.at[b], x_peer(d))

    def residual_wait(b):
        await_bytes(rbuf.at[b, 0:3], rr.at[b])

    def solve(b):
        residual = rbuf[b].reshape(1024, COLS)

        def rows(number):
            width = (number + 1) * QUARTER
            left = ibuf[b, number, :, :, :, :width].reshape(QUARTER, width)
            wbuf[b, number] = dot(left, residual[:width]).astype(BF)

        if FULL[b]:
            for number in range(NX):
                rows(number)
        else:
            by_x(rows)

    def share(b):
        for d in range(1, NX):
            send(wbuf.at[b, x], wbuf.at[b, x], ws.at[b], wr.at[b], x_peer(d))

    def share_wait(b):
        await_bytes(wbuf.at[b, 0:3], wr.at[b])

    def spread(b):
        dst = obuf.at[z, b]
        local(wbuf.at[b, x, own_rows, :], dst, orr.at[b])

        def step(d, carry):
            other = (z + d) % NZ
            send(
                wbuf.at[b, x, rows_of(other), :],
                dst,
                os.at[b],
                orr.at[b],
                (g, x * NZ + other),
            )
            return carry

        lax.fori_loop(1, NZ, step, 0)

    def update(j, b):
        parts = [mbufs[b][k % 2, k // 2, j + 1] for k in range(8)]
        panel = jnp.concatenate(parts, axis=1)
        kbuf[b] = kbuf[b] - dot(panel, wbuf[j].reshape(1024, COLS))

    def make_pickers():
        source = lax.broadcasted_iota(jnp.int32, (512, 128), 0)
        target = lax.broadcasted_iota(jnp.int32, (512, 128), 1)
        for chunk in range(NX):
            wanted = (target // 32) * 128 + chunk * 32 + target % 32
            pick[chunk] = jnp.where(source == wanted, 1.0, 0.0).astype(BF)

    def assemble(b):
        await_bytes(obuf.at[:, b], orr.at[b])
        for half in range(2):
            rows = jnp.concatenate([obuf[half * 4 + k, b] for k in range(4)], axis=1)
            for chunk in range(NX):
                at = (chunk * 2 + half) * 128
                out[b, :, at : at + 128] = dot(rows, pick[chunk]).astype(BF)

    barrier = pltpu.get_barrier_semaphore()
    peers = [x_peer(d) for d in range(1, NX)] + [y_peer(d) for d in range(1, NY)]
    peers += [z_peer(d) for d in range(1, NZ)] + [core_peer]
    for peer in peers:
        pl.semaphore_signal(barrier, inc=1, device_id=peer, device_id_type=MESH)
    def own_inv(b):
        def go(number):
            width = (number + 1) * QUARTER
            half = pl.ds(pl.multiple_of(c * 16, 16), 16)
            local(inv.at[b, half, :width], ibuf.at[b, number, z, c, :, :width], own_sem.at[b])

        by_x(go)

    def own_row(b):
        sem = own_sem.at[4 + b]
        local(lab.at[b], mbufs[b].at[c, y, 0, own_rows, :], sem)
        for j in range(b):
            cols = pl.ds(pl.multiple_of(j * 1024 + g * 128, 128), 128)
            local(fac.at[b, :, cols], mbufs[b].at[c, y, j + 1, own_rows, :], sem)

    own_row(0)
    local(cand, cbuf.at[x], own_sem.at[8])
    for b in range(4):
        own_inv(b)
        if b < 3:
            own_row(b + 1)
    pl.semaphore_wait(barrier, len(peers))

    i0, i1, i2, i3 = [("inv", b) for b in range(4)]
    m1, m2, m3 = [("row", b) for b in range(1, 4)]
    make_pickers()

    row_first()
    await_bytes(cbuf.at[x], own_sem.at[8])
    for d in range(1, NX):
        send(cbuf.at[x], cbuf.at[x], cs, cr, x_peer(d))
    begin(i0)
    begin(m1)
    begin(i1)
    relay(i0)
    relay(m1)
    row_y(0)
    begin(m2)
    inv_x(0)
    row_y(1)
    relay(i1)
    begin(i2)
    row_relay(0, 1)
    row_relay(0, 3)
    row_core(0)
    await_bytes(cbuf.at[0:3], cr)
    relay(m2)
    begin(m3)
    row_wait(0)
    make_kernel(0)
    publish(0)
    relay(i2)
    inv_x(1)
    begin(i3)
    row_relay(1, 1)
    row_relay(1, 3)
    row_core(1)
    row_y(2)
    inv_relay(0, 1)
    inv_relay(0, 3)
    inv_core(0)
    relay(m3)
    relay(i3)
    row_wait(1)
    make_kernel(1)
    inv_wait(0)
    residual_wait(0)
    solve(0)
    spread(0)
    update(0, 1)
    publish(1)
    inv_x(2)
    row_relay(2, 1)
    row_relay(2, 3)
    row_y(3)
    row_core(2)
    row_wait(2)
    make_kernel(2)
    update(0, 2)
    inv_wait(1)
    residual_wait(1)
    solve(1)
    share(1)
    spread(1)
    share_wait(1)
    update(1, 2)
    publish(2)
    row_relay(3, 1)
    row_relay(3, 3)
    inv_x(3)
    row_core(3)
    row_wait(3)
    make_kernel(3)
    update(0, 3)
    update(1, 3)
    inv_wait(2)
    residual_wait(2)
    solve(2)
    share(2)
    spread(2)
    share_wait(2)
    update(2, 3)
    publish(3)

    for b in range(3):
        assemble(b)
    await_bytes(mbuf0.at[c, y, :, 0:224, :], m1s)
    for b in range(4):
        if b > 0:
            await_bytes(mbufs[b].at[c, y, :, 0:224, :], zs.at[ITEMS.index(("row", b))])
        await_bytes(mbufs[b].at[c, 0:3], m2s.at[b])
        await_bytes(mbufs[b].at[c], m3s.at[b])
    await_bytes(cbuf.at[0:3], cs)
    def owed(number):
        for b in range(4):
            await_bytes(inv_part(b, number, c, 0, 7), zs.at[ITEMS.index(("inv", b))])
            if FULL[b]:
                for _ in X_STEPS[b]:
                    await_bytes(inv_part(b, number, c), i2s.at[b])
                if len(X_STEPS[b]) == 2:
                    await_bytes(inv_part(b, (number - 1) % NX, c, 0, 4), i2s.at[b])
                    await_bytes(inv_part(b, (number + 1) % NX, c, 4, 8), i2s.at[b])

    by_x(owed)
    for b in range(4):
        if FULL[b]:
            for number in range(NX):
                await_bytes(inv_part(b, number, c), i3s.at[b])
        else:
            by_x(lambda number: await_bytes(inv_part(b, number, c), i3s.at[b]))
            if b < 3:
                await_bytes(wbuf.at[b, 0:3], ws.at[b])
    total = jnp.zeros((1, COLS), jnp.float32)
    for b in range(3):
        values = wbuf[b, x].astype(jnp.float32)
        total = total + jnp.sum(values * values, axis=0, keepdims=True)
    inv_wait(3)
    residual_wait(3)
    solve(3)
    spread(3)

    tail = wbuf[3, x].astype(jnp.float32)
    epart[r] = total + jnp.sum(tail * tail, axis=0, keepdims=True)

    def tell(d, carry):
        other = (r + d) % (NX * NZ)
        send(epart.at[r], epart.at[r], es, er, (g, other))
        return carry

    lax.fori_loop(1, NX * NZ, tell, 0)
    assemble(3)

    await_bytes(epart.at[0:31], er)
    esum = [sum(epart[k + NZ * i] for i in range(1, NX)) + epart[k] for k in range(NZ)]
    lane = lax.broadcasted_iota(jnp.int32, (1, 128), 1) // 32
    for chunk in range(NX):
        for half in range(2):
            row = jnp.zeros((1, COLS), jnp.float32)
            for k in range(4):
                moved = pltpu.roll(esum[half * 4 + k], ((k - chunk) % 4) * 32, 1)
                row = jnp.where(lane == k, moved, row)
            expl[chunk * 2 + half : chunk * 2 + half + 1, :] = row

    for b in range(4):
        await_bytes(rbuf.at[b, 0:3], rs.at[b])
        await_bytes(obuf.at[0:7, b], os.at[b])
    await_bytes(epart.at[0:31], es)


def on_device(labeled, candidates, factor_rows, block_inverse):
    dma = pltpu.SemaphoreType.DMA
    scale = 0.5 / math.sqrt(1024)
    whitened, explained = pl.pallas_call(
        functools.partial(kernel, scale),
        out_shape=(
            jax.ShapeDtypeStruct((4, 32, 1024), BF),
            jax.ShapeDtypeStruct((8, 128), jnp.float32),
        ),
        in_specs=[pl.BlockSpec(memory_space=pltpu.HBM)] * 4,
        out_specs=(
            pl.BlockSpec(memory_space=pltpu.VMEM),
            pl.BlockSpec(memory_space=pltpu.VMEM),
        ),
        scratch_shapes=[
            pltpu.VMEM((2, NY, 1, QUARTER, 128), BF),
            pltpu.VMEM((2, NY, 2, QUARTER, 128), BF),
            pltpu.VMEM((2, NY, 3, QUARTER, 128), BF),
            pltpu.VMEM((2, NY, 4, QUARTER, 128), BF),
            pltpu.VMEM((NX, 32, 1024), BF),
            pltpu.VMEM((4, NX, NZ, 2, 16, 1024), BF),
            pltpu.VMEM((4, QUARTER, COLS), jnp.float32),
            pltpu.VMEM((4, NX, QUARTER, COLS), BF),
            pltpu.VMEM((4, NX, QUARTER, COLS), BF),
            pltpu.VMEM((NZ, 4, 32, COLS), BF),
            pltpu.VMEM((NX, 512, 128), BF),
            pltpu.VMEM((NX * NZ, 1, COLS), jnp.float32),
            dma((9,)),
            dma((8,)),
            dma((8, 3)),
            dma,
            dma,
            dma((4,)),
            dma((4, NY)),
            dma((4,)),
            dma((4,)),
            dma,
            dma,
            dma((3,)),
            dma((3, NX)),
            dma((4,)),
            dma((4, NX)),
            dma((4,)),
            dma((4,)),
            dma((3,)),
            dma((3,)),
            dma((4,)),
            dma((4,)),
            dma,
            dma,
        ],
        compiler_params=pltpu.CompilerParams(
            collective_id=0, has_side_effects=True, vmem_limit_bytes=VMEM_BYTES
        ),
        name="whiten",
    )(labeled, candidates, factor_rows, block_inverse)
    return whitened, explained.reshape(1024)


def solution(mesh):
    in_specs = (
        P(None, "row", "grp"),
        P(("grp", "row"), None),
        P(None, "row", None),
        P(None, "row", None),
    )
    out_specs = (P(None, "row", "grp"), P("grp"))
    return jax.shard_map(
        on_device, mesh=mesh, in_specs=in_specs, out_specs=out_specs, check_vma=False
    )
```

```python
import functools
import math

import jax
import jax.numpy as jnp
from jax import lax
from jax.experimental import pallas as pl
from jax.experimental.pallas import tpu as pltpu
from jax.sharding import PartitionSpec as P

MESH = pl.DeviceIdType.MESH
BF = jnp.bfloat16
NX, NY, NZ = 4, 4, 8
QUARTER = 256
COLS = 128
VMEM_BYTES = 63 * 1024 * 1024
ITEMS = [("inv", 0), ("inv", 1), ("inv", 2), ("inv", 3)]
ITEMS += [("row", 0), ("row", 1), ("row", 2), ("row", 3)]
Z_DIRECT = ()
FULL = (True, False, False, False)
Y_STEPS = ((1, 3, 2), (1, 3, 2), (1, 3, 2), (1, 3, 2))
X_STEPS = ((1, 3), (1, 3), (1, 3))


def dot(a, b):
    return jnp.dot(a, b, preferred_element_type=jnp.float32)


def kernel(
    scale,
    lab,
    cand,
    fac,
    inv,
    out,
    expl,
    mbuf0,
    mbuf1,
    mbuf2,
    mbuf3,
    cbuf,
    ibuf,
    kbuf,
    rbuf,
    wbuf,
    obuf,
    pick,
    epart,
    own_sem,
    zs,
    zr,
    m1s,
    m1r,
    m2s,
    m2r,
    m3s,
    m3r,
    cs,
    cr,
    i2s,
    i2r,
    i3s,
    i3r,
    rs,
    rr,
    ws,
    wr,
    os,
    orr,
    es,
    er,
):
    g = lax.axis_index("grp")
    r = lax.axis_index("row")
    y, c = g // 2, g % 2
    x, z = r // NZ, r % NZ
    mbufs = (mbuf0, mbuf1, mbuf2, mbuf3)

    def x_peer(d):
        return (g, ((x + d) % NX) * NZ + z)

    def y_peer(d):
        return (((y + d) % NY) * 2 + c, r)

    def z_peer(d):
        return (g, x * NZ + (z + d) % NZ)

    core_peer = (y * 2 + 1 - c, r)

    def send(src, dst, ssem, rsem, device):
        pltpu.make_async_remote_copy(
            src_ref=src,
            dst_ref=dst,
            send_sem=ssem,
            recv_sem=rsem,
            device_id=device,
            device_id_type=MESH,
        ).start()

    def local(src, dst, sem):
        pltpu.make_async_copy(src, dst, sem).start()

    def await_bytes(ref, sem):
        pltpu.make_async_copy(ref, ref, sem).wait()

    def each_z(body):
        def step(d, carry):
            body(z_peer(d))
            return carry

        lax.fori_loop(1, NZ, step, 0)

    def rows_of(position):
        return pl.ds(pl.multiple_of(position * 32, 32), 32)

    own_rows = rows_of(z)

    side = 1 - 2 * c

    def along(distance):
        return (z + NZ + distance) % NZ

    def z_at(distance):
        return (g, x * NZ + along(distance))

    def slots(item, first, count):
        rows = pl.ds(pl.multiple_of(first * 32, 32), count * 32)
        return mbufs[item[1]].at[c, y, :, rows, :]

    def inv_slots(b, number, first, count):
        width = (number + 1) * QUARTER
        return ibuf.at[b, number, pl.ds(first, count), c, :, :width]

    def at_slots(item, body):
        if item[0] == "inv":
            by_x(lambda number: body(functools.partial(inv_slots, item[1], number)))
        else:
            body(functools.partial(slots, item))

    def by_x(body):
        for number in range(NX):
            pl.when(x == number)(functools.partial(body, number))

    def begin(item):
        n = ITEMS.index(item)

        def go(at):
            own = at(z, 1)
            await_bytes(own, own_sem.at[n])
            if item in Z_DIRECT:
                each_z(lambda peer: send(own, own, zs.at[n], zr.at[n, 0], peer))
                return
            for distance in (2, -2, 1, -1):
                near = 0 if abs(distance) == 2 else 1
                send(own, own, zs.at[n], zr.at[n, near], z_at(distance))

        at_slots(item, go)

    def relay(item):
        n = ITEMS.index(item)
        if item in Z_DIRECT:
            return

        def go(at):
            await_bytes(at(0, 2), zr.at[n, 0])
            for distance in (2, -2):
                one = at(along(-distance), 1)
                send(one, one, zs.at[n], zr.at[n, 2], z_at(distance // 2))
            far = at(along(-2 * side), 1)
            send(far, far, zs.at[n], zr.at[n, 2], z_at(2 * side))

        at_slots(item, go)

    def arrive(item):
        n = ITEMS.index(item)

        def go(at):
            if item in Z_DIRECT:
                await_bytes(at(0, 7), zr.at[n, 0])
                return
            await_bytes(at(0, 2), zr.at[n, 1])
            await_bytes(at(0, 3), zr.at[n, 2])

        at_slots(item, go)

    def row_first():
        own = slots(("row", 0), z, 1)
        await_bytes(own, own_sem.at[ITEMS.index(("row", 0))])
        each_z(lambda peer: send(own, own, m1s, m1r, peer))

    def row_y(b):
        block = mbufs[b].at[c, y]
        if b == 0:
            await_bytes(mbuf0.at[c, y, :, 0:224, :], m1r)
        else:
            arrive(("row", b))
        for d in Y_STEPS[b]:
            send(block, block, m2s.at[b], m2r.at[b, d], y_peer(d))

    def row_relay(b, step):
        lo = 0 if step == 1 else 128
        other = (y + NY - step) % NY
        await_bytes(mbufs[b].at[c, other], m2r.at[b, step])
        if len(Y_STEPS[b]) == 2:
            half = mbufs[b].at[c, other, :, lo : lo + 128, :]
            send(half, half, m2s.at[b], m2r.at[b, 2], y_peer(step))

    def row_core(b):
        await_bytes(mbufs[b].at[c, 0], m2r.at[b, 2])
        half = mbufs[b].at[c]
        send(half, half, m3s.at[b], m3r.at[b], core_peer)

    def row_wait(b):
        await_bytes(mbufs[b].at[1 - c], m3r.at[b])

    def inv_part(b, number, core, lo=0, hi=NZ):
        return ibuf.at[b, number, lo:hi, core, :, : (number + 1) * QUARTER]

    def inv_across(b, number):
        part = inv_part(b, number, c)
        send(part, part, i3s.at[b], i3r.at[b, number], core_peer)

    def inv_x(b):
        arrive(("inv", b))

        def go(number):
            part = inv_part(b, number, c)
            if FULL[b]:
                for d in X_STEPS[b]:
                    send(part, part, i2s.at[b], i2r.at[b, number], x_peer(d))
            inv_across(b, number)

        by_x(go)

    def inv_relay(b, step):
        lo = 0 if step == 1 else 4

        def go(number):
            other = (number + NX - step) % NX
            await_bytes(inv_part(b, other, c), i2r.at[b, other])
            if len(X_STEPS[b]) == 2:
                half = inv_part(b, other, c, lo, lo + 4)
                send(half, half, i2s.at[b], i2r.at[b, other], x_peer(step))
            inv_across(b, other)

        by_x(go)

    def inv_core(b):
        def go(number):
            far = (number + 2) % NX
            await_bytes(inv_part(b, far, c), i2r.at[b, far])
            inv_across(b, far)

        by_x(go)

    def inv_wait(b):
        if FULL[b]:
            for number in range(NX):
                await_bytes(inv_part(b, number, 1 - c), i3r.at[b, number])
        else:
            by_x(lambda number: await_bytes(inv_part(b, number, 1 - c), i3r.at[b, number]))

    def make_kernel(b):
        rows = jnp.concatenate([mbufs[b][k % 2, k // 2, 0] for k in range(8)], axis=1)
        sums = lax.dot_general(
            rows,
            cbuf[...].reshape(COLS, 1024),
            (((1,), (1,)), ((), ())),
            preferred_element_type=jnp.float32,
        )
        kbuf[b] = jnp.exp(sums * scale)

    def publish(b):
        rbuf[b, x] = kbuf[b].astype(BF)
        own = rbuf.at[b, x]
        if FULL[b]:
            for d in range(1, NX):
                send(own, own, rs.at[b], rr.at[b], x_peer(d))
        else:

            def below(number):
                for other in range(NX - 1, number, -1):
                    send(own, own, rs.at[b], rr.at[b], (g, other * NZ + z))

            by_x(below)

    def residual_wait(b):
        if FULL[b]:
            await_bytes(rbuf.at[b, 0:3], rr.at[b])
        else:

            def above(number):
                if number:
                    await_bytes(rbuf.at[b, 0:number], rr.at[b])

            by_x(above)

    def solve(b):
        def rows(number):
            width = (number + 1) * QUARTER
            left = ibuf[b, number, :, :, :, :width].reshape(QUARTER, width)
            residual = rbuf[b, : number + 1].reshape(width, COLS)
            wbuf[b, number] = dot(left, residual).astype(BF)

        if FULL[b]:
            for number in range(NX):
                rows(number)
        else:
            by_x(rows)

    def share(b):
        for d in range(1, NX):
            send(wbuf.at[b, x], wbuf.at[b, x], ws.at[b], wr.at[b], x_peer(d))

    def share_wait(b):
        await_bytes(wbuf.at[b, 0:3], wr.at[b])

    def spread(b):
        dst = obuf.at[z, b]
        local(wbuf.at[b, x, own_rows, :], dst, orr.at[b])

        def step(d, carry):
            other = (z + d) % NZ
            send(
                wbuf.at[b, x, rows_of(other), :],
                dst,
                os.at[b],
                orr.at[b],
                (g, x * NZ + other),
            )
            return carry

        lax.fori_loop(1, NZ, step, 0)

    def update(j, b):
        parts = [mbufs[b][k % 2, k // 2, j + 1] for k in range(8)]
        panel = jnp.concatenate(parts, axis=1)
        kbuf[b] = kbuf[b] - dot(panel, wbuf[j].reshape(1024, COLS))

    def make_pickers():
        source = lax.broadcasted_iota(jnp.int32, (512, 128), 0)
        target = lax.broadcasted_iota(jnp.int32, (512, 128), 1)
        for chunk in range(NX):
            wanted = (target // 32) * 128 + chunk * 32 + target % 32
            pick[chunk] = jnp.where(source == wanted, 1.0, 0.0).astype(BF)

    def assemble(b):
        await_bytes(obuf.at[:, b], orr.at[b])
        for half in range(2):
            rows = jnp.concatenate([obuf[half * 4 + k, b] for k in range(4)], axis=1)
            for chunk in range(NX):
                at = (chunk * 2 + half) * 128
                out[b, :, at : at + 128] = dot(rows, pick[chunk]).astype(BF)

    barrier = pltpu.get_barrier_semaphore()
    peers = [x_peer(d) for d in range(1, NX)] + [y_peer(d) for d in range(1, NY)]
    peers += [z_peer(d) for d in range(1, NZ)] + [core_peer]
    for peer in peers:
        pl.semaphore_signal(barrier, inc=1, device_id=peer, device_id_type=MESH)
    def own_inv(b):
        def go(number):
            width = (number + 1) * QUARTER
            half = pl.ds(pl.multiple_of(c * 16, 16), 16)
            local(inv.at[b, half, :width], ibuf.at[b, number, z, c, :, :width], own_sem.at[b])

        by_x(go)

    def own_row(b):
        sem = own_sem.at[4 + b]
        local(lab.at[b], mbufs[b].at[c, y, 0, own_rows, :], sem)
        for j in range(b):
            cols = pl.ds(pl.multiple_of(j * 1024 + g * 128, 128), 128)
            local(fac.at[b, :, cols], mbufs[b].at[c, y, j + 1, own_rows, :], sem)

    own_row(0)
    local(cand, cbuf.at[x], own_sem.at[8])
    for b in range(4):
        own_inv(b)
        if b < 3:
            own_row(b + 1)
    pl.semaphore_wait(barrier, len(peers))

    i0, i1, i2, i3 = [("inv", b) for b in range(4)]
    m1, m2, m3 = [("row", b) for b in range(1, 4)]
    make_pickers()

    row_first()
    await_bytes(cbuf.at[x], own_sem.at[8])
    for d in range(1, NX):
        send(cbuf.at[x], cbuf.at[x], cs, cr, x_peer(d))
    begin(i0)
    begin(m1)
    begin(i1)
    relay(i0)
    relay(m1)
    row_y(0)
    begin(m2)
    inv_x(0)
    row_y(1)
    relay(i1)
    begin(i2)
    row_relay(0, 1)
    row_relay(0, 3)
    row_core(0)
    await_bytes(cbuf.at[0:3], cr)
    relay(m2)
    begin(m3)
    row_wait(0)
    make_kernel(0)
    publish(0)
    relay(i2)
    inv_x(1)
    begin(i3)
    row_relay(1, 1)
    row_relay(1, 3)
    row_core(1)
    row_y(2)
    inv_relay(0, 1)
    inv_relay(0, 3)
    inv_core(0)
    relay(m3)
    relay(i3)
    row_wait(1)
    make_kernel(1)
    inv_wait(0)
    residual_wait(0)
    solve(0)
    spread(0)
    update(0, 1)
    publish(1)
    inv_x(2)
    row_relay(2, 1)
    row_relay(2, 3)
    row_y(3)
    row_core(2)
    row_wait(2)
    make_kernel(2)
    update(0, 2)
    inv_wait(1)
    residual_wait(1)
    solve(1)
    share(1)
    spread(1)
    share_wait(1)
    update(1, 2)
    publish(2)
    row_relay(3, 1)
    row_relay(3, 3)
    inv_x(3)
    row_core(3)
    row_wait(3)
    make_kernel(3)
    update(0, 3)
    update(1, 3)
    inv_wait(2)
    residual_wait(2)
    solve(2)
    share(2)
    spread(2)
    share_wait(2)
    update(2, 3)
    publish(3)

    for b in range(3):
        assemble(b)
    await_bytes(mbuf0.at[c, y, :, 0:224, :], m1s)
    for b in range(4):
        if b > 0:
            await_bytes(mbufs[b].at[c, y, :, 0:224, :], zs.at[ITEMS.index(("row", b))])
        await_bytes(mbufs[b].at[c, 0:3], m2s.at[b])
        await_bytes(mbufs[b].at[c], m3s.at[b])
    await_bytes(cbuf.at[0:3], cs)
    def owed(number):
        for b in range(4):
            await_bytes(inv_part(b, number, c, 0, 7), zs.at[ITEMS.index(("inv", b))])
            if FULL[b]:
                for _ in X_STEPS[b]:
                    await_bytes(inv_part(b, number, c), i2s.at[b])
                if len(X_STEPS[b]) == 2:
                    await_bytes(inv_part(b, (number - 1) % NX, c, 0, 4), i2s.at[b])
                    await_bytes(inv_part(b, (number + 1) % NX, c, 4, 8), i2s.at[b])

    by_x(owed)
    for b in range(4):
        if FULL[b]:
            for number in range(NX):
                await_bytes(inv_part(b, number, c), i3s.at[b])
        else:
            by_x(lambda number: await_bytes(inv_part(b, number, c), i3s.at[b]))
            if b < 3:
                await_bytes(wbuf.at[b, 0:3], ws.at[b])
    total = jnp.zeros((1, COLS), jnp.float32)
    for b in range(3):
        values = wbuf[b, x].astype(jnp.float32)
        total = total + jnp.sum(values * values, axis=0, keepdims=True)
    inv_wait(3)
    residual_wait(3)
    solve(3)
    spread(3)

    tail = wbuf[3, x].astype(jnp.float32)
    epart[r] = total + jnp.sum(tail * tail, axis=0, keepdims=True)

    def tell(d, carry):
        other = (r + d) % (NX * NZ)
        send(epart.at[r], epart.at[r], es, er, (g, other))
        return carry

    lax.fori_loop(1, NX * NZ, tell, 0)
    assemble(3)

    await_bytes(epart.at[0:31], er)
    esum = [sum(epart[k + NZ * i] for i in range(1, NX)) + epart[k] for k in range(NZ)]
    lane = lax.broadcasted_iota(jnp.int32, (1, 128), 1) // 32
    for chunk in range(NX):
        for half in range(2):
            row = jnp.zeros((1, COLS), jnp.float32)
            for k in range(4):
                moved = pltpu.roll(esum[half * 4 + k], ((k - chunk) % 4) * 32, 1)
                row = jnp.where(lane == k, moved, row)
            expl[chunk * 2 + half : chunk * 2 + half + 1, :] = row

    for b in range(4):
        if FULL[b]:
            await_bytes(rbuf.at[b, 0:3], rs.at[b])
        else:

            def sent(number):
                if number < NX - 1:
                    await_bytes(rbuf.at[b, 0 : NX - 1 - number], rs.at[b])

            by_x(sent)
        await_bytes(obuf.at[0:7, b], os.at[b])
    await_bytes(epart.at[0:31], es)


def on_device(labeled, candidates, factor_rows, block_inverse):
    dma = pltpu.SemaphoreType.DMA
    scale = 0.5 / math.sqrt(1024)
    whitened, explained = pl.pallas_call(
        functools.partial(kernel, scale),
        out_shape=(
            jax.ShapeDtypeStruct((4, 32, 1024), BF),
            jax.ShapeDtypeStruct((8, 128), jnp.float32),
        ),
        in_specs=[pl.BlockSpec(memory_space=pltpu.HBM)] * 4,
        out_specs=(
            pl.BlockSpec(memory_space=pltpu.VMEM),
            pl.BlockSpec(memory_space=pltpu.VMEM),
        ),
        scratch_shapes=[
            pltpu.VMEM((2, NY, 1, QUARTER, 128), BF),
            pltpu.VMEM((2, NY, 2, QUARTER, 128), BF),
            pltpu.VMEM((2, NY, 3, QUARTER, 128), BF),
            pltpu.VMEM((2, NY, 4, QUARTER, 128), BF),
            pltpu.VMEM((NX, 32, 1024), BF),
            pltpu.VMEM((4, NX, NZ, 2, 16, 1024), BF),
            pltpu.VMEM((4, QUARTER, COLS), jnp.float32),
            pltpu.VMEM((4, NX, QUARTER, COLS), BF),
            pltpu.VMEM((4, NX, QUARTER, COLS), BF),
            pltpu.VMEM((NZ, 4, 32, COLS), BF),
            pltpu.VMEM((NX, 512, 128), BF),
            pltpu.VMEM((NX * NZ, 1, COLS), jnp.float32),
            dma((9,)),
            dma((8,)),
            dma((8, 3)),
            dma,
            dma,
            dma((4,)),
            dma((4, NY)),
            dma((4,)),
            dma((4,)),
            dma,
            dma,
            dma((3,)),
            dma((3, NX)),
            dma((4,)),
            dma((4, NX)),
            dma((4,)),
            dma((4,)),
            dma((3,)),
            dma((3,)),
            dma((4,)),
            dma((4,)),
            dma,
            dma,
        ],
        compiler_params=pltpu.CompilerParams(
            collective_id=0, has_side_effects=True, vmem_limit_bytes=VMEM_BYTES
        ),
        name="whiten",
    )(labeled, candidates, factor_rows, block_inverse)
    return whitened, explained.reshape(1024)


def solution(mesh):
    in_specs = (
        P(None, "row", "grp"),
        P(("grp", "row"), None),
        P(None, "row", None),
        P(None, "row", None),
    )
    out_specs = (P(None, "row", "grp"), P("grp"))
    return jax.shard_map(
        on_device, mesh=mesh, in_specs=in_specs, out_specs=out_specs, check_vma=False
    )
```

```python
import functools
import math

import jax
import jax.numpy as jnp
from jax import lax
from jax.experimental import pallas as pl
from jax.experimental.pallas import tpu as pltpu
from jax.sharding import PartitionSpec as P

MESH = pl.DeviceIdType.MESH
BF = jnp.bfloat16
NX, NY, NZ = 4, 4, 8
QUARTER = 256
COLS = 128
VMEM_BYTES = 63 * 1024 * 1024
ITEMS = [("inv", 0), ("inv", 1), ("inv", 2), ("inv", 3)]
ITEMS += [("row", 0), ("row", 1), ("row", 2), ("row", 3)]
Z_DIRECT = ()
FULL = (True, False, False, False)
Y_STEPS = ((1, 3, 2), (1, 3, 2), (1, 3, 2), (1, 3, 2))
X_STEPS = ((1, 3), (1, 3), (1, 3))


def dot(a, b):
    return jnp.dot(a, b, preferred_element_type=jnp.float32)


def kernel(
    scale,
    lab,
    cand,
    fac,
    inv,
    out,
    expl,
    mbuf0,
    mbuf1,
    mbuf2,
    mbuf3,
    cbuf,
    ibuf,
    kbuf,
    rbuf,
    wbuf,
    obuf,
    pick,
    epart,
    own_sem,
    zs,
    zr,
    m1s,
    m1r,
    m2s,
    m2r,
    m3s,
    m3r,
    cs,
    cr,
    i2s,
    i2r,
    i3s,
    i3r,
    rs,
    rr,
    ws,
    wr,
    os,
    orr,
    es,
    er,
):
    g = lax.axis_index("grp")
    r = lax.axis_index("row")
    y, c = g // 2, g % 2
    x, z = r // NZ, r % NZ
    mbufs = (mbuf0, mbuf1, mbuf2, mbuf3)

    def x_peer(d):
        return (g, ((x + d) % NX) * NZ + z)

    def y_peer(d):
        return (((y + d) % NY) * 2 + c, r)

    def z_peer(d):
        return (g, x * NZ + (z + d) % NZ)

    core_peer = (y * 2 + 1 - c, r)

    def send(src, dst, ssem, rsem, device):
        pltpu.make_async_remote_copy(
            src_ref=src,
            dst_ref=dst,
            send_sem=ssem,
            recv_sem=rsem,
            device_id=device,
            device_id_type=MESH,
        ).start()

    def local(src, dst, sem):
        pltpu.make_async_copy(src, dst, sem).start()

    def await_bytes(ref, sem):
        pltpu.make_async_copy(ref, ref, sem).wait()

    def each_z(body):
        def step(d, carry):
            body(z_peer(d))
            return carry

        lax.fori_loop(1, NZ, step, 0)

    def rows_of(position):
        return pl.ds(pl.multiple_of(position * 32, 32), 32)

    own_rows = rows_of(z)

    side = 1 - 2 * c

    def along(distance):
        return (z + NZ + distance) % NZ

    def z_at(distance):
        return (g, x * NZ + along(distance))

    def slots(item, first, count):
        rows = pl.ds(pl.multiple_of(first * 32, 32), count * 32)
        return mbufs[item[1]].at[c, y, :, rows, :]

    def inv_slots(b, number, first, count):
        width = (number + 1) * QUARTER
        return ibuf.at[b, number, pl.ds(first, count), c, :, :width]

    def at_slots(item, body):
        if item[0] == "inv":
            by_x(lambda number: body(functools.partial(inv_slots, item[1], number)))
        else:
            body(functools.partial(slots, item))

    def by_x(body):
        for number in range(NX):
            pl.when(x == number)(functools.partial(body, number))

    def begin(item):
        n = ITEMS.index(item)

        def go(at):
            own = at(z, 1)
            await_bytes(own, own_sem.at[n])
            if item in Z_DIRECT:
                each_z(lambda peer: send(own, own, zs.at[n], zr.at[n, 0], peer))
                return
            for distance in (2, -2, 1, -1):
                near = 0 if abs(distance) == 2 else 1
                send(own, own, zs.at[n], zr.at[n, near], z_at(distance))

        at_slots(item, go)

    def relay(item):
        n = ITEMS.index(item)
        if item in Z_DIRECT:
            return

        def go(at):
            await_bytes(at(0, 2), zr.at[n, 0])
            for distance in (2, -2):
                one = at(along(-distance), 1)
                send(one, one, zs.at[n], zr.at[n, 2], z_at(distance // 2))
            far = at(along(-2 * side), 1)
            send(far, far, zs.at[n], zr.at[n, 2], z_at(2 * side))

        at_slots(item, go)

    def arrive(item):
        n = ITEMS.index(item)

        def go(at):
            if item in Z_DIRECT:
                await_bytes(at(0, 7), zr.at[n, 0])
                return
            await_bytes(at(0, 2), zr.at[n, 1])
            await_bytes(at(0, 3), zr.at[n, 2])

        at_slots(item, go)

    def row_first():
        own = slots(("row", 0), z, 1)
        await_bytes(own, own_sem.at[ITEMS.index(("row", 0))])
        each_z(lambda peer: send(own, own, m1s, m1r, peer))

    def row_y(b):
        block = mbufs[b].at[c, y]
        if b == 0:
            await_bytes(mbuf0.at[c, y, :, 0:224, :], m1r)
        else:
            arrive(("row", b))
        for d in Y_STEPS[b]:
            send(block, block, m2s.at[b], m2r.at[b, d], y_peer(d))

    def row_relay(b, step):
        lo = 0 if step == 1 else 128
        other = (y + NY - step) % NY
        await_bytes(mbufs[b].at[c, other], m2r.at[b, step])
        if len(Y_STEPS[b]) == 2:
            half = mbufs[b].at[c, other, :, lo : lo + 128, :]
            send(half, half, m2s.at[b], m2r.at[b, 2], y_peer(step))

    def row_core(b):
        await_bytes(mbufs[b].at[c, 0], m2r.at[b, 2])
        half = mbufs[b].at[c]
        send(half, half, m3s.at[b], m3r.at[b], core_peer)

    def row_wait(b):
        await_bytes(mbufs[b].at[1 - c], m3r.at[b])

    def inv_part(b, number, core, lo=0, hi=NZ):
        return ibuf.at[b, number, lo:hi, core, :, : (number + 1) * QUARTER]

    def inv_across(b, number):
        part = inv_part(b, number, c)
        send(part, part, i3s.at[b], i3r.at[b, number], core_peer)

    def inv_x(b):
        arrive(("inv", b))

        def go(number):
            part = inv_part(b, number, c)
            if FULL[b]:
                for d in X_STEPS[b]:
                    send(part, part, i2s.at[b], i2r.at[b, number], x_peer(d))
            inv_across(b, number)

        by_x(go)

    def inv_relay(b, step):
        lo = 0 if step == 1 else 4

        def go(number):
            other = (number + NX - step) % NX
            await_bytes(inv_part(b, other, c), i2r.at[b, other])
            if len(X_STEPS[b]) == 2:
                half = inv_part(b, other, c, lo, lo + 4)
                send(half, half, i2s.at[b], i2r.at[b, other], x_peer(step))
            inv_across(b, other)

        by_x(go)

    def inv_core(b):
        def go(number):
            far = (number + 2) % NX
            await_bytes(inv_part(b, far, c), i2r.at[b, far])
            inv_across(b, far)

        by_x(go)

    def inv_wait(b):
        if FULL[b]:
            for number in range(NX):
                await_bytes(inv_part(b, number, 1 - c), i3r.at[b, number])
        else:
            by_x(lambda number: await_bytes(inv_part(b, number, 1 - c), i3r.at[b, number]))

    def make_kernel(b):
        rows = jnp.concatenate([mbufs[b][k % 2, k // 2, 0] for k in range(8)], axis=1)
        sums = lax.dot_general(
            rows,
            cbuf[...].reshape(COLS, 1024),
            (((1,), (1,)), ((), ())),
            preferred_element_type=jnp.float32,
        )
        kbuf[b] = jnp.exp(sums * scale)

    def publish(b):
        rbuf[b, x] = kbuf[b].astype(BF)
        own = rbuf.at[b, x]
        if FULL[b]:
            for d in range(1, NX):
                send(own, own, rs.at[b], rr.at[b], x_peer(d))
        else:

            def below(number):
                for other in range(NX - 1, number, -1):
                    send(own, own, rs.at[b], rr.at[b], (g, other * NZ + z))

            by_x(below)

    def residual_wait(b):
        if FULL[b]:
            await_bytes(rbuf.at[b, 0:3], rr.at[b])
        else:

            def above(number):
                if number:
                    await_bytes(rbuf.at[b, 0:number], rr.at[b])

            by_x(above)

    def solve(b):
        def rows(number):
            width = (number + 1) * QUARTER
            left = ibuf[b, number, :, :, :, :width].reshape(QUARTER, width)
            residual = rbuf[b, : number + 1].reshape(width, COLS)
            wbuf[b, number] = dot(left, residual).astype(BF)

        if FULL[b]:
            for number in range(NX):
                rows(number)
        else:
            by_x(rows)

    def share(b):
        for d in range(1, NX):
            send(wbuf.at[b, x], wbuf.at[b, x], ws.at[b], wr.at[b], x_peer(d))

    def share_wait(b):
        await_bytes(wbuf.at[b, 0:3], wr.at[b])

    def spread(b):
        dst = obuf.at[z, b]
        local(wbuf.at[b, x, own_rows, :], dst, orr.at[b])

        def step(d, carry):
            other = (z + d) % NZ
            send(
                wbuf.at[b, x, rows_of(other), :],
                dst,
                os.at[b],
                orr.at[b],
                (g, x * NZ + other),
            )
            return carry

        lax.fori_loop(1, NZ, step, 0)

    def update(j, b):
        parts = [mbufs[b][k % 2, k // 2, j + 1] for k in range(8)]
        panel = jnp.concatenate(parts, axis=1)
        kbuf[b] = kbuf[b] - dot(panel, wbuf[j].reshape(1024, COLS))

    def make_pickers():
        source = lax.broadcasted_iota(jnp.int32, (512, 128), 0)
        target = lax.broadcasted_iota(jnp.int32, (512, 128), 1)
        for chunk in range(NX):
            wanted = (target // 32) * 128 + chunk * 32 + target % 32
            pick[chunk] = jnp.where(source == wanted, 1.0, 0.0).astype(BF)

    def assemble(b):
        await_bytes(obuf.at[:, b], orr.at[b])
        for half in range(2):
            rows = jnp.concatenate([obuf[half * 4 + k, b] for k in range(4)], axis=1)
            for chunk in range(NX):
                at = (chunk * 2 + half) * 128
                out[b, :, at : at + 128] = dot(rows, pick[chunk]).astype(BF)

    barrier = pltpu.get_barrier_semaphore()
    peers = [x_peer(d) for d in range(1, NX)] + [y_peer(d) for d in range(1, NY)]
    peers += [z_peer(d) for d in range(1, NZ)] + [core_peer]
    for peer in peers:
        pl.semaphore_signal(barrier, inc=1, device_id=peer, device_id_type=MESH)
    def own_inv(b):
        def go(number):
            width = (number + 1) * QUARTER
            half = pl.ds(pl.multiple_of(c * 16, 16), 16)
            local(inv.at[b, half, :width], ibuf.at[b, number, z, c, :, :width], own_sem.at[b])

        by_x(go)

    def own_row(b):
        sem = own_sem.at[4 + b]
        local(lab.at[b], mbufs[b].at[c, y, 0, own_rows, :], sem)
        for j in range(b):
            cols = pl.ds(pl.multiple_of(j * 1024 + g * 128, 128), 128)
            local(fac.at[b, :, cols], mbufs[b].at[c, y, j + 1, own_rows, :], sem)

    own_row(0)
    local(cand, cbuf.at[x], own_sem.at[8])
    for b in range(4):
        own_inv(b)
        if b < 3:
            own_row(b + 1)
    pl.semaphore_wait(barrier, len(peers))

    i0, i1, i2, i3 = [("inv", b) for b in range(4)]
    m1, m2, m3 = [("row", b) for b in range(1, 4)]
    make_pickers()

    row_first()
    await_bytes(cbuf.at[x], own_sem.at[8])
    for d in range(1, NX):
        send(cbuf.at[x], cbuf.at[x], cs, cr, x_peer(d))
    begin(i0)
    begin(m1)
    begin(i1)
    relay(i0)
    relay(m1)
    row_y(0)
    begin(m2)
    inv_x(0)
    row_y(1)
    relay(i1)
    begin(i2)
    row_relay(0, 1)
    row_relay(0, 3)
    row_core(0)
    await_bytes(cbuf.at[0:3], cr)
    relay(m2)
    begin(m3)
    row_wait(0)
    make_kernel(0)
    publish(0)
    relay(i2)
    inv_x(1)
    begin(i3)
    row_relay(1, 1)
    row_relay(1, 3)
    row_core(1)
    row_y(2)
    inv_relay(0, 1)
    inv_relay(0, 3)
    inv_core(0)
    relay(m3)
    relay(i3)
    row_wait(1)
    make_kernel(1)
    inv_wait(0)
    residual_wait(0)
    solve(0)
    spread(0)
    update(0, 1)
    publish(1)
    inv_x(2)
    row_relay(2, 1)
    row_relay(2, 3)
    row_y(3)
    row_core(2)
    row_wait(2)
    make_kernel(2)
    update(0, 2)
    inv_wait(1)
    residual_wait(1)
    solve(1)
    share(1)
    spread(1)
    share_wait(1)
    update(1, 2)
    publish(2)
    row_relay(3, 1)
    row_relay(3, 3)
    inv_x(3)
    row_core(3)
    row_wait(3)
    make_kernel(3)
    update(0, 3)
    update(1, 3)
    inv_wait(2)
    residual_wait(2)
    solve(2)
    share(2)
    spread(2)
    share_wait(2)
    update(2, 3)
    publish(3)

    for b in range(3):
        assemble(b)
    await_bytes(mbuf0.at[c, y, :, 0:224, :], m1s)
    for b in range(4):
        if b > 0:
            await_bytes(mbufs[b].at[c, y, :, 0:224, :], zs.at[ITEMS.index(("row", b))])
        await_bytes(mbufs[b].at[c, 0:3], m2s.at[b])
        await_bytes(mbufs[b].at[c], m3s.at[b])
    await_bytes(cbuf.at[0:3], cs)
    def owed(number):
        for b in range(4):
            await_bytes(inv_part(b, number, c, 0, 7), zs.at[ITEMS.index(("inv", b))])
            if FULL[b]:
                for _ in X_STEPS[b]:
                    await_bytes(inv_part(b, number, c), i2s.at[b])
                if len(X_STEPS[b]) == 2:
                    await_bytes(inv_part(b, (number - 1) % NX, c, 0, 4), i2s.at[b])
                    await_bytes(inv_part(b, (number + 1) % NX, c, 4, 8), i2s.at[b])

    by_x(owed)
    for b in range(4):
        if FULL[b]:
            for number in range(NX):
                await_bytes(inv_part(b, number, c), i3s.at[b])
        else:
            by_x(lambda number: await_bytes(inv_part(b, number, c), i3s.at[b]))
            if b < 3:
                await_bytes(wbuf.at[b, 0:3], ws.at[b])
    total = jnp.zeros((1, COLS), jnp.float32)
    for b in range(3):
        values = wbuf[b, x].astype(jnp.float32)
        total = total + jnp.sum(values * values, axis=0, keepdims=True)
    inv_wait(3)
    residual_wait(3)
    solve(3)

    tail = wbuf[3, x].astype(jnp.float32)
    epart[r] = total + jnp.sum(tail * tail, axis=0, keepdims=True)

    def tell(d, carry):
        other = (r + d) % (NX * NZ)
        send(epart.at[r], epart.at[r], es, er, (g, other))
        return carry

    lax.fori_loop(1, NX * NZ, tell, 0)
    spread(3)
    assemble(3)

    await_bytes(epart.at[0:31], er)
    esum = [sum(epart[k + NZ * i] for i in range(1, NX)) + epart[k] for k in range(NZ)]
    lane = lax.broadcasted_iota(jnp.int32, (1, 128), 1) // 32
    for chunk in range(NX):
        for half in range(2):
            row = jnp.zeros((1, COLS), jnp.float32)
            for k in range(4):
                moved = pltpu.roll(esum[half * 4 + k], ((k - chunk) % 4) * 32, 1)
                row = jnp.where(lane == k, moved, row)
            expl[chunk * 2 + half : chunk * 2 + half + 1, :] = row

    for b in range(4):
        if FULL[b]:
            await_bytes(rbuf.at[b, 0:3], rs.at[b])
        else:

            def sent(number):
                if number < NX - 1:
                    await_bytes(rbuf.at[b, 0 : NX - 1 - number], rs.at[b])

            by_x(sent)
        await_bytes(obuf.at[0:7, b], os.at[b])
    await_bytes(epart.at[0:31], es)


def on_device(labeled, candidates, factor_rows, block_inverse):
    dma = pltpu.SemaphoreType.DMA
    scale = 0.5 / math.sqrt(1024)
    whitened, explained = pl.pallas_call(
        functools.partial(kernel, scale),
        out_shape=(
            jax.ShapeDtypeStruct((4, 32, 1024), BF),
            jax.ShapeDtypeStruct((8, 128), jnp.float32),
        ),
        in_specs=[pl.BlockSpec(memory_space=pltpu.HBM)] * 4,
        out_specs=(
            pl.BlockSpec(memory_space=pltpu.VMEM),
            pl.BlockSpec(memory_space=pltpu.VMEM),
        ),
        scratch_shapes=[
            pltpu.VMEM((2, NY, 1, QUARTER, 128), BF),
            pltpu.VMEM((2, NY, 2, QUARTER, 128), BF),
            pltpu.VMEM((2, NY, 3, QUARTER, 128), BF),
            pltpu.VMEM((2, NY, 4, QUARTER, 128), BF),
            pltpu.VMEM((NX, 32, 1024), BF),
            pltpu.VMEM((4, NX, NZ, 2, 16, 1024), BF),
            pltpu.VMEM((4, QUARTER, COLS), jnp.float32),
            pltpu.VMEM((4, NX, QUARTER, COLS), BF),
            pltpu.VMEM((4, NX, QUARTER, COLS), BF),
            pltpu.VMEM((NZ, 4, 32, COLS), BF),
            pltpu.VMEM((NX, 512, 128), BF),
            pltpu.VMEM((NX * NZ, 1, COLS), jnp.float32),
            dma((9,)),
            dma((8,)),
            dma((8, 3)),
            dma,
            dma,
            dma((4,)),
            dma((4, NY)),
            dma((4,)),
            dma((4,)),
            dma,
            dma,
            dma((3,)),
            dma((3, NX)),
            dma((4,)),
            dma((4, NX)),
            dma((4,)),
            dma((4,)),
            dma((3,)),
            dma((3,)),
            dma((4,)),
            dma((4,)),
            dma,
            dma,
        ],
        compiler_params=pltpu.CompilerParams(
            collective_id=0, has_side_effects=True, vmem_limit_bytes=VMEM_BYTES
        ),
        name="whiten",
    )(labeled, candidates, factor_rows, block_inverse)
    return whitened, explained.reshape(1024)


def solution(mesh):
    in_specs = (
        P(None, "row", "grp"),
        P(("grp", "row"), None),
        P(None, "row", None),
        P(None, "row", None),
    )
    out_specs = (P(None, "row", "grp"), P("grp"))
    return jax.shard_map(
        on_device, mesh=mesh, in_specs=in_specs, out_specs=out_specs, check_vma=False
    )
```
